512 devices in a mesh: dp: 8 (over x, core), space: 64 (over z, y).
Axes of the slice: x: 4, y: 4, z: 16, core: 2. Of those that a mesh axis runs over, the one named last changes fastest.
Arguments:
- features: bfloat16 [8, 65536, 256], P('dp', 'space'), may hold values from -6 to 6
- weight: bfloat16 [2048, 256], P(('dp', 'space')), may hold values from -0.125 to 0.125
- rulebook: int32 [8, 512, 3, 8], P('dp', 'space'), may hold values from 0 to 63, as said below
- rule_counts: int32 [8, 512], P('dp', 'space'), may hold values from 1 to 8, as said below
- cotangent: bfloat16 [8, 32768, 256], P('dp', 'space'), may hold values from -6 to 6
Outputs:
- activated: bfloat16 [8, 32768, 256], P('dp', 'space')
- grad_features: bfloat16 [8, 65536, 256], P('dp', 'space')
- grad_weight: float32 [2048, 256], P(('dp', 'space'))
The draws below stay inside these ranges and needn't reach their ends.
Inputs may be any that keep to these rules, and one draw needn't show every extreme that they name: `rulebook`: in the row of slab s the owner is s - 1, s or s + 1 and lies in 0 to 63; the input block lies in 0 to 7; the output block lies in 0 to 3, and in 2 to 3 when the owner is s - 1, in 0 to 1 when it is s + 1. Padded slots hold entries of the same kind. A block may appear in several rules. `rule_counts`: some slab and offset has 8 live rules in every draw.
All inputs are finite; a program needn't handle non-finite values.
Results may differ from the reference program's by a relative error of at most 0.0049.
Values may be sent and summed in bfloat16 or wider, within the bound.
A program may use at most 64 MiB of HBM per device.

```python
import jax
import jax.numpy as jnp
from jax import lax

CI = 256
CO = 256
OFFS = 8
BR = 128
BND = 2
SLOTS = 8
IN_BLK = 8
OUT_BLK = 4
SCENES = 8
N_SPACE = 64


def draw_rulebook(key, part):
    key = jax.random.fold_in(key, 11)
    first, second, third, fourth = jax.random.split(key, 4)
    shape = (SCENES, N_SPACE * OFFS, SLOTS)
    device = lax.broadcasted_iota(jnp.int32, shape, 1) // OFFS
    in_index = jax.random.randint(first, shape, 0, IN_BLK)
    code = jax.random.randint(second, shape, 0, 4)
    relative = jnp.where(code == 0, -1, jnp.where(code == 3, 1, 0))
    relative = jnp.where(device + relative < 0, 0, relative)
    relative = jnp.where(device + relative > N_SPACE - 1, 0, relative)
    inner = jax.random.randint(third, shape, 0, OUT_BLK)
    rim = jax.random.randint(fourth, shape, 0, BND)
    out_index = jnp.where(relative == 0, inner, jnp.where(relative < 0, OUT_BLK - BND + rim, rim))
    return jnp.stack([in_index, out_index, device + relative], axis=2).astype(jnp.int32)


def draw_rule_counts(key, part):
    key = jax.random.fold_in(key, 23)
    first, second, third, fourth = jax.random.split(key, 4)
    heavy = jax.random.randint(first, (SCENES, N_SPACE, 1), 0, 4) == 0
    high = jax.random.randint(second, (SCENES, N_SPACE, OFFS), SLOTS // 2, SLOTS + 1)
    low = jax.random.randint(third, (SCENES, N_SPACE, OFFS), 1, SLOTS // 2 + 1)
    counts = jnp.where(heavy, high, low).reshape(SCENES, N_SPACE * OFFS)
    chosen = jax.random.randint(fourth, (), 0, SCENES * N_SPACE * OFFS)
    flat = lax.broadcasted_iota(jnp.int32, (SCENES, N_SPACE * OFFS), 0) * (N_SPACE * OFFS) + lax.broadcasted_iota(jnp.int32, (SCENES, N_SPACE * OFFS), 1)
    return jnp.where(flat == chosen, SLOTS, counts).astype(jnp.int32)


def shard_levels(rng, extent, pieces, low, largest):
    def one(position, blocks):
        draws = jax.random.uniform(jax.random.fold_in(jax.random.fold_in(rng, 6), position), (blocks,), jnp.float32, low / len(pieces), largest / len(pieces))
        return jnp.repeat(jnp.exp(draws), extent[position] // blocks).reshape((-1,) + (1,) * (len(extent) - position - 1))

    loudness = one(*pieces[0])
    for cut in pieces[1:]:
        loudness = loudness * one(*cut)
    return loudness


def noise(stream_key, shape, scale, most, cuts=(), kind=jnp.bfloat16):
    drawn = jax.random.normal(stream_key, shape, jnp.float32) * scale
    if len(cuts) > 0:
        drawn = shard_levels(stream_key, shape, cuts, -0.22, 0.18) * drawn
    return jnp.clip(drawn, min=-most, max=most).astype(kind)


def setup_inputs(seed: int = 0) -> dict:
    key_of = jax.random.split(jax.random.key(seed), 6)
    features = noise(key_of[0], (SCENES, N_SPACE * IN_BLK * BR, CI), 1.0, 6.0, ((0, 8), (1, 64)))
    weight = noise(key_of[1], (OFFS * CI, CO), (OFFS * CI) ** -0.5, 0.125, ((0, 512),))
    rulebook = draw_rulebook(jax.random.fold_in(key_of[5], 71), 0)
    rule_counts = draw_rule_counts(jax.random.fold_in(key_of[5], 71), 0)
    cotangent = noise(key_of[4], (SCENES, N_SPACE * OUT_BLK * BR, CO), 1.0, 6.0, ((0, 8), (1, 64)))
    return {"features": features, "weight": weight, "rulebook": rulebook, "rule_counts": rule_counts, "cotangent": cotangent}


grad_scale = 1.0 / 2048.0


def reference(features, weight, rulebook, rule_counts, cotangent):
    kernel = weight.reshape(OFFS, CI, CO)
    slot_ids = jnp.arange(SLOTS, dtype=jnp.int32)
    slab_ids = jnp.arange(N_SPACE, dtype=jnp.int32)
    total_in = N_SPACE * IN_BLK
    total_out = N_SPACE * OUT_BLK
    grad_total = jnp.zeros((OFFS, CI, CO), jnp.float32)
    outs_act = []
    outs_grad = []
    for scene in range(SCENES):
        blocks = features[scene].reshape(total_in, BR, CI)
        rules = rulebook[scene].reshape(N_SPACE, OFFS, 3, SLOTS)
        counts = rule_counts[scene].reshape(N_SPACE, OFFS)
        in_global = (rules[:, :, 0, :] + slab_ids[:, None, None] * IN_BLK).astype(jnp.int32)
        out_global = (rules[:, :, 2, :] * OUT_BLK + rules[:, :, 1, :]).astype(jnp.int32)
        live = slot_ids[None, None, :] < counts[:, :, None]
        in_off = jnp.transpose(in_global, (1, 0, 2)).reshape(OFFS, N_SPACE * SLOTS)
        out_off = jnp.transpose(out_global, (1, 0, 2)).reshape(OFFS, N_SPACE * SLOTS)
        live_off = jnp.transpose(live, (1, 0, 2)).reshape(OFFS, N_SPACE * SLOTS)

        def forward_step(carry, item):
            in_idx, out_idx, alive, kern = item
            picked = blocks[in_idx].reshape(N_SPACE * SLOTS * BR, CI)
            prod = jnp.dot(picked, kern, preferred_element_type=jnp.float32)
            prod = prod.reshape(N_SPACE * SLOTS, BR, CO) * alive.astype(jnp.float32)[:, None, None]
            return carry + jax.ops.segment_sum(prod, out_idx, num_segments=total_out), None

        pre, _ = lax.scan(forward_step, jnp.zeros((total_out, BR, CO), jnp.float32), (in_off, out_off, live_off, kernel))
        sigma = jax.nn.sigmoid(pre)
        activated = (pre * sigma).astype(jnp.bfloat16)
        upstream = cotangent[scene].reshape(total_out, BR, CO).astype(jnp.float32)
        grad_pre = (upstream * sigma * (1.0 + pre * (1.0 - sigma))).astype(jnp.bfloat16)

        def backward_step(carry, item):
            in_idx, out_idx, alive, kern = item
            rule_grads = grad_pre[out_idx] * alive.astype(jnp.bfloat16)[:, None, None]
            rule_flat = rule_grads.reshape(N_SPACE * SLOTS * BR, CO)
            back = jnp.dot(rule_flat, kern.T, preferred_element_type=jnp.float32)
            back = back.reshape(N_SPACE * SLOTS, BR, CI)
            picked = blocks[in_idx].reshape(N_SPACE * SLOTS * BR, CI)
            term = jnp.dot(picked.T, rule_flat, preferred_element_type=jnp.float32)
            return carry + jax.ops.segment_sum(back, in_idx, num_segments=total_in), term

        grad_in, terms = lax.scan(backward_step, jnp.zeros((total_in, BR, CI), jnp.float32), (in_off, out_off, live_off, kernel))
        grad_total = grad_total + terms
        outs_act.append(activated.reshape(total_out * BR, CO))
        outs_grad.append(grad_in.astype(jnp.bfloat16).reshape(total_in * BR, CI))
    grad_weight = (grad_total * grad_scale).reshape(OFFS * CI, CO)
    return jnp.stack(outs_act, 0), jnp.stack(outs_grad, 0), grad_weight
```

```python
import functools

import jax
import jax.numpy as jnp
from jax import lax
from jax.experimental import pallas as pl
from jax.experimental.pallas import tpu as pltpu
from jax.sharding import PartitionSpec as P

OFFS = 8
BND = 2
SLOTS = 8
IN_BLK = 8
OUT_BLK = 4
EXT = OUT_BLK + 2 * BND
NONE = OFFS * SLOTS

grad_scale = 1.0 / 2048.0
BF16 = jnp.bfloat16
F32 = jnp.float32
MESH = pl.DeviceIdType.MESH

NX, NY, NZ = 4, 4, 16


def dot(a, b, dims):
    return lax.dot_general(a, b, (dims, ((), ())), preferred_element_type=F32)


NN = ((1,), (0,))
NT = ((1,), (1,))


def kernel(
    feat_hbm, w_ref, rules, counts, cot_hbm,
    act_hbm, gf_hbm, gw_ref,
    xin, xp, xt, cot, wz, wst, wf, yb, sums, hs, hr, gext, act, gfp,
    sb_send, sb_recv, own, xs, xr, ys, yr, zs, zr,
    f_in, f_prev, b_slot, b_prev, lasts,
    loc_sem, z_sem, y_sem, x_sem, c_sem, h_sem, rc_sem, rx_sem, ry_sem, rz_sem,
):
    ci = xin.shape[1]
    br = xp.shape[1]
    dp = lax.axis_index("dp")
    space = lax.axis_index("space")
    x, c = lax.div(dp, 2), lax.rem(dp, 2)
    z, y = lax.div(space, NY), lax.rem(space, NY)
    oc = 1 - c
    n_space = NY * NZ
    sib = (x * 2 + oc, space)
    up = (dp, lax.rem(space + 1, n_space))
    down = (dp, lax.rem(space + n_space - 1, n_space))

    def x_of(off):
        return lax.rem(x + off, NX)

    def at_x(off):
        return (x_of(off) * 2 + c, space)

    def at_y(off):
        return (dp, z * NY + lax.rem(y + off, NY))

    def at_z(off):
        return (dp, lax.rem(z + off, NZ) * NY + y)

    def remote(src, dst, sems, index, device):
        return pltpu.make_async_remote_copy(
            src_ref=src, dst_ref=dst, send_sem=sems.at[0, index], recv_sem=sems.at[1, index],
            device_id=device, device_id_type=MESH,
        )

    get_x = pltpu.make_async_copy(feat_hbm.at[0], xin, loc_sem.at[0])
    get_cot = pltpu.make_async_copy(cot_hbm.at[0], cot, loc_sem.at[1])
    get_x.start()
    get_cot.start()
    barrier = pltpu.get_barrier_semaphore()

    def greet(device):
        pl.semaphore_signal(barrier, inc=1, device_id=device, device_id_type=MESH)

    wz[0, 0:4, :] = w_ref[:, 0:128].astype(F32)
    wz[0, 4:8, :] = w_ref[:, 128:256].astype(F32)

    @pl.loop(1, NZ)
    def _(d):
        greet(at_z(d))

    for d in range(1, NY):
        greet(at_y(d))
    for d in range(1, NX):
        greet(at_x(d))
    for device in (sib, up, down):
        greet(device)
    pl.semaphore_wait(barrier, NZ + NY + NX)

    @pl.loop(1, NZ)
    def _(d):
        remote(wz.at[0], wz.at[d], z_sem, d, at_z(d)).start()

    get_x.wait()
    rows = lax.broadcasted_iota(jnp.int32, (ci, ci), 0)
    cols = lax.broadcasted_iota(jnp.int32, (ci, ci), 1)

    def channel(p):
        from_y = lax.rem(y + NY - lax.div(p, 4 * NZ), NY)
        from_z = lax.rem(z + NZ - lax.div(lax.rem(p, 4 * NZ), 4), NZ)
        return from_z * (4 * NY) + from_y * 4 + lax.rem(p, 4)

    perm = jnp.where(rows == channel(cols), 1.0, 0.0).astype(BF16)
    perm_t = jnp.where(cols == channel(rows), 1.0, 0.0).astype(BF16)

    @pl.loop(0, IN_BLK)
    def _(i):
        block = xin[pl.ds(pl.multiple_of(i * br, br), br), :]
        xp[i] = dot(block, perm, NN).astype(BF16)
        xt[i] = dot(perm_t, block, NT).astype(BF16)

    sums[NONE] = jnp.zeros(sums.shape[1:], F32)
    gext[EXT] = jnp.zeros(gext.shape[1:], BF16)

    def kernel_at(t):
        pair = t // 2
        off = pair + (pair // 2) * (1 - 2 * (pair % 2))
        return lax.rem(x + off, NX) * 2 + lax.rem(c + t % 2, 2)

    def chain(t, carry):
        f_last, b_last = list(carry[:EXT]), list(carry[EXT:])
        k = kernel_at(t)
        count = counts[0, k]
        for j in range(SLOTS):
            n = t * SLOTS + j
            source, block, owner = rules[0, k, 0, j], rules[0, k, 1, j], rules[0, k, 2, j]
            slot = BND + block + (owner - space) * OUT_BLK
            live = j < count
            slot = jnp.where(live, slot, EXT)
            start = jnp.where(live, source, IN_BLK)
            f_in[n] = source
            b_slot[n] = slot
            prev = jnp.int32(NONE)
            for o in range(EXT):
                hit = slot == o
                prev = jnp.where(hit, f_last[o], prev)
                f_last[o] = jnp.where(hit, n, f_last[o])
            f_prev[n] = prev
            prev = jnp.int32(NONE)
            for o in range(IN_BLK):
                hit = start == o
                prev = jnp.where(hit, b_last[o], prev)
                b_last[o] = jnp.where(hit, n, b_last[o])
            b_prev[n] = prev
        return tuple(f_last + b_last)

    ends = lax.fori_loop(0, OFFS, chain, (jnp.int32(NONE),) * (EXT + IN_BLK))
    for o in range(EXT + IN_BLK):
        lasts[o] = ends[o]

    @pl.loop(1, NZ)
    def _(d):
        remote(wz.at[0], wz.at[d], z_sem, d, at_z(d)).wait_recv()

    low = lax.broadcasted_iota(jnp.int32, (8, 128), 0) < 4
    for p in range(NZ // 2):
        a, b = wz[2 * p], wz[2 * p + 1]
        wst[8 * p : 8 * p + 8, 0:128] = jnp.where(low, a, pltpu.roll(b, 4, 0))
        wst[8 * p : 8 * p + 8, 128:256] = jnp.where(low, pltpu.roll(a, 4, 0), b)
    part = 4 * NZ
    wf[0, 0:part, :] = wst[...].astype(BF16)

    def y_copy(d):
        return remote(wf.at[0, pl.ds(0, part)], wf.at[0, pl.ds(d * part, part)], y_sem, d, at_y(d))

    for d in range(1, NY):
        y_copy(d).start()
    for d in range(1, NY):
        y_copy(d).wait_recv()

    order = (0, 1, 3, 2)

    def x_copy(d):
        return remote(wf.at[0], wf.at[2 * order.index(NX - d)], x_sem, d, at_x(d))

    def c_copy(off):
        t = 2 * order.index(off)
        return remote(wf.at[t], wf.at[t + 1], c_sem, off, sib)

    for d in (1, 3, 2):
        x_copy(d).start()
    c_copy(0).start()

    def arrive(off, other):
        if other:
            c_copy(off).wait_recv()
        elif off:
            x_copy(NX - off).wait_recv()
            c_copy(off).start()

    for t in range(OFFS):
        arrive(order[t // 2], t % 2 == 1)
        flat = xp[...].reshape(IN_BLK * br, ci)
        yb[...] = dot(flat, wf[t], NN).reshape(yb.shape)
        for j in range(SLOTS):
            n = t * SLOTS + j
            sums[n] = yb[f_in[n]] + sums[f_prev[n]]

    for i in range(BND):
        hs[i] = sums[lasts[i]].astype(BF16)
        hs[BND + i] = sums[lasts[BND + OUT_BLK + i]].astype(BF16)
    low_rim, high_rim = pl.ds(0, BND), pl.ds(BND, BND)
    remote(hs.at[low_rim], hr.at[high_rim], h_sem, 0, down).start()
    remote(hs.at[high_rim], hr.at[low_rim], h_sem, 1, up).start()
    get_cot.wait()
    remote(hs.at[high_rim], hr.at[low_rim], h_sem, 1, up).wait_recv()
    remote(hs.at[low_rim], hr.at[high_rim], h_sem, 0, down).wait_recv()
    for o in range(OUT_BLK):
        pre = sums[lasts[BND + o]] + hr[o].astype(F32)
        sigma = jax.nn.sigmoid(pre)
        act[o * br : (o + 1) * br, :] = (pre * sigma).astype(BF16)
        upstream = cot[o * br : (o + 1) * br, :].astype(F32)
        gext[BND + o] = (upstream * sigma * (1.0 + pre * (1.0 - sigma))).astype(BF16)
    own_low, own_high = pl.ds(BND, BND), pl.ds(OUT_BLK, BND)
    top, bottom = pl.ds(BND + OUT_BLK, BND), pl.ds(0, BND)
    remote(gext.at[own_low], gext.at[top], h_sem, 2, down).start()
    remote(gext.at[own_high], gext.at[bottom], h_sem, 3, up).start()
    put_act = pltpu.make_async_copy(act, act_hbm.at[0], loc_sem.at[2])
    put_act.start()
    remote(gext.at[own_low], gext.at[top], h_sem, 2, down).wait_recv()
    remote(gext.at[own_high], gext.at[bottom], h_sem, 3, up).wait_recv()

    def term(off, other):
        t = 2 * order.index(off) + int(other)
        lhs = [xt[f_in[t * SLOTS + j]] for j in range(SLOTS)]
        rhs = [gext[b_slot[t * SLOTS + j]] for j in range(SLOTS)]
        return dot(jnp.concatenate(lhs, axis=1), jnp.concatenate(rhs, axis=0), NN)

    def to_sibling(off):
        sb_send[off] = term(off, True)
        remote(sb_send.at[off], sb_recv.at[off], rc_sem, off, sib).start()

    sequence = (2, 1, 3, 0)
    to_sibling(sequence[0])
    for i, off in enumerate(sequence):
        own[...] = term(off, False)
        if i + 1 < NX:
            to_sibling(sequence[i + 1])
        remote(sb_send.at[off], sb_recv.at[off], rc_sem, off, sib).wait_recv()
        if off:
            xs[off] = (own[...] + sb_recv[off]).astype(BF16)
            remote(xs.at[off], xr.at[off], rx_sem, off, at_x(off)).start()
        else:
            own[...] += sb_recv[off]

    for t in range(OFFS):
        flat = gext[0:EXT].reshape(EXT * br, gext.shape[2])
        yb[:, :, 0:ci] = dot(flat, wf[t], NT).reshape(EXT, br, ci)
        for j in range(SLOTS):
            n = t * SLOTS + j
            place = jnp.minimum(b_slot[n], EXT - 1)
            sums[n] = yb[place] + sums[b_prev[n]]

    for d in range(1, NX):
        remote(xs.at[d], xr.at[d], rx_sem, d, at_x(d)).wait_recv()
    total = own[...]
    for d in range(1, NX):
        total = total + xr[d].astype(F32)
    own[...] = total
    for d in range(1, NY):
        ys[d] = own[(NY - d) * part : (NY - d + 1) * part, :].astype(BF16)
        remote(ys.at[d], yr.at[d], ry_sem, d, at_y(d)).start()

    for i in range(IN_BLK):
        back = sums[lasts[EXT + i]][:, 0:ci].astype(BF16)
        gfp[i * br : (i + 1) * br, :] = dot(back, perm_t, NN).astype(BF16)
    put_gf = pltpu.make_async_copy(gfp, gf_hbm.at[0], loc_sem.at[3])
    put_gf.start()

    for d in range(1, NY):
        remote(ys.at[d], yr.at[d], ry_sem, d, at_y(d)).wait_recv()
    total = own[0:part, :]
    for d in range(1, NY):
        total = total + yr[d].astype(F32)
    for p in range(NZ // 2):
        a, b = total[8 * p : 8 * p + 8, 0:128], total[8 * p : 8 * p + 8, 128:256]
        zs[2 * p] = jnp.where(low, a, pltpu.roll(b, 4, 0))
        zs[2 * p + 1] = jnp.where(low, pltpu.roll(a, 4, 0), b)

    @pl.loop(1, NZ)
    def _(d):
        remote(zs.at[NZ - d], zr.at[d], rz_sem, d, at_z(d)).start()

    @pl.loop(1, NZ)
    def _(d):
        remote(zs.at[NZ - d], zr.at[d], rz_sem, d, at_z(d)).wait_recv()

    total = zs[0]
    for d in range(1, NZ):
        total = total + zr[d]
    total = total * grad_scale
    gw_ref[:, 0:128] = total[0:4]
    gw_ref[:, 128:256] = total[4:8]

    @pl.loop(1, NZ)
    def _(d):
        remote(wz.at[0], wz.at[d], z_sem, d, at_z(d)).wait_send()
        remote(zs.at[NZ - d], zr.at[d], rz_sem, d, at_z(d)).wait_send()

    for d in range(1, NY):
        y_copy(d).wait_send()
        remote(ys.at[d], yr.at[d], ry_sem, d, at_y(d)).wait_send()
    for d in range(1, NX):
        x_copy(d).wait_send()
        remote(xs.at[d], xr.at[d], rx_sem, d, at_x(d)).wait_send()
    for off in range(NX):
        c_copy(off).wait_send()
        remote(sb_send.at[off], sb_recv.at[off], rc_sem, off, sib).wait_send()
    remote(hs.at[low_rim], hr.at[high_rim], h_sem, 0, down).wait_send()
    remote(hs.at[high_rim], hr.at[low_rim], h_sem, 1, up).wait_send()
    remote(gext.at[own_low], gext.at[top], h_sem, 2, down).wait_send()
    remote(gext.at[own_high], gext.at[bottom], h_sem, 3, up).wait_send()
    put_act.wait()
    put_gf.wait()


def local(features, weight, rulebook, rule_counts, cotangent):
    ci, co = features.shape[2], weight.shape[1]
    br = features.shape[1] // IN_BLK
    vmem = pl.BlockSpec(memory_space=pltpu.VMEM)
    smem = pl.BlockSpec(memory_space=pltpu.SMEM)
    hbm = pl.BlockSpec(memory_space=pl.ANY)
    dma = pltpu.SemaphoreType.DMA
    V = pltpu.VMEM
    return pl.pallas_call(
        kernel,
        out_shape=(
            jax.ShapeDtypeStruct(cotangent.shape, BF16),
            jax.ShapeDtypeStruct(features.shape, BF16),
            jax.ShapeDtypeStruct(weight.shape, F32),
        ),
        in_specs=[hbm, vmem, smem, smem, hbm],
        out_specs=(hbm, hbm, vmem),
        scratch_shapes=[
            V((IN_BLK * br, ci), BF16),
            V((IN_BLK, br, ci), BF16),
            V((IN_BLK, ci, br), BF16),
            V((OUT_BLK * br, co), BF16),
            V((NZ, 8, 128), F32),
            V((4 * NZ, co), F32),
            V((OFFS, ci, co), BF16),
            V((IN_BLK, br, max(ci, co)), F32),
            V((NONE + 1, br, max(ci, co)), F32),
            V((2 * BND, br, co), BF16),
            V((2 * BND, br, co), BF16),
            V((EXT + 1, br, co), BF16),
            V((OUT_BLK * br, co), BF16),
            V((IN_BLK * br, ci), BF16),
            V((NX, ci, co), F32),
            V((NX, ci, co), F32),
            V((ci, co), F32),
            V((NX, ci, co), BF16),
            V((NX, ci, co), BF16),
            V((NY, 4 * NZ, co), BF16),
            V((NY, 4 * NZ, co), BF16),
            V((NZ, 8, 128), F32),
            V((NZ, 8, 128), F32),
            pltpu.SMEM((NONE,), jnp.int32),
            pltpu.SMEM((NONE,), jnp.int32),
            pltpu.SMEM((NONE,), jnp.int32),
            pltpu.SMEM((NONE,), jnp.int32),
            pltpu.SMEM((EXT + IN_BLK,), jnp.int32),
            dma((4,)),
            dma((2, NZ)),
            dma((2, NY)),
            dma((2, NX)),
            dma((2, NX)),
            dma((2, 4)),
            dma((2, NX)),
            dma((2, NX)),
            dma((2, NY)),
            dma((2, NZ)),
        ],
        compiler_params=pltpu.CompilerParams(
            collective_id=0, has_side_effects=True, vmem_limit_bytes=48 * 1024 * 1024
        ),
    )(features, weight, rulebook, rule_counts, cotangent)


def solution(mesh):
    in_specs = (
        P("dp", "space", None),
        P(("dp", "space"), None),
        P("dp", "space", None, None),
        P("dp", "space"),
        P("dp", "space", None),
    )
    out_specs = (P("dp", "space", None), P("dp", "space", None), P(("dp", "space"), None))
    return jax.shard_map(local, mesh=mesh, in_specs=in_specs, out_specs=out_specs, check_vma=False)
```

```python
import functools

import jax
import jax.numpy as jnp
from jax import lax
from jax.experimental import pallas as pl
from jax.experimental.pallas import tpu as pltpu
from jax.sharding import PartitionSpec as P

OFFS = 8
BND = 2
SLOTS = 8
IN_BLK = 8
OUT_BLK = 4
EXT = OUT_BLK + 2 * BND
NONE = OFFS * SLOTS

grad_scale = 1.0 / 2048.0
BF16 = jnp.bfloat16
F32 = jnp.float32
MESH = pl.DeviceIdType.MESH

NX, NY, NZ = 4, 4, 16
REACH = 4


def dot(a, b, dims):
    return lax.dot_general(a, b, (dims, ((), ())), preferred_element_type=F32)


NN = ((1,), (0,))
NT = ((1,), (1,))


def kernel(
    feat_hbm, w_hbm, rules_hbm, counts_hbm, cot_hbm,
    act_hbm, gf_hbm, gw_hbm,
    xin, win, rules, counts, xp, xt, cot, wz, wst, wf, yb, sums, hs, hr, gext, act_ref, gf_ref, gw_ref,
    sb_send, sb_recv, own, xs, xr, ys, yr, zs, zr,
    f_in, f_prev, b_slot, b_prev, lasts,
    loc_sem, z_sem, y_sem, x_sem, c_sem, h_sem, rc_sem, rx_sem, ry_sem, rz_sem,
):
    ci = xin.shape[2]
    br = xp.shape[1]
    dp = lax.axis_index("dp")
    space = lax.axis_index("space")
    x, c = lax.div(dp, 2), lax.rem(dp, 2)
    z, y = lax.div(space, NY), lax.rem(space, NY)
    oc = 1 - c
    n_space = NY * NZ
    sib = (x * 2 + oc, space)
    up = (dp, lax.rem(space + 1, n_space))
    down = (dp, lax.rem(space + n_space - 1, n_space))

    def x_of(off):
        return lax.rem(x + off, NX)

    def at_x(off):
        return (x_of(off) * 2 + c, space)

    def at_y(off):
        return (dp, z * NY + lax.rem(y + off, NY))

    def at_z(off):
        return (dp, lax.rem(z + off, NZ) * NY + y)

    def remote(src, dst, sems, index, device):
        return pltpu.make_async_remote_copy(
            src_ref=src, dst_ref=dst, send_sem=sems.at[0, index], recv_sem=sems.at[1, index],
            device_id=device, device_id_type=MESH,
        )

    pending = []

    def send(copy):
        copy.start()
        pending.append(copy.wait_send)

    def put(src, dst, index):
        copy = pltpu.make_async_copy(src, dst, loc_sem.at[index])
        copy.start()
        pending.append(copy.wait)

    get_w = pltpu.make_async_copy(w_hbm, win, loc_sem.at[0])
    get_x = pltpu.make_async_copy(feat_hbm, xin, loc_sem.at[1])
    get_rules = pltpu.make_async_copy(rules_hbm, rules, loc_sem.at[2])
    get_counts = pltpu.make_async_copy(counts_hbm, counts, loc_sem.at[3])
    get_cot = pltpu.make_async_copy(cot_hbm.at[0], cot.at[pl.ds(BND, OUT_BLK)], loc_sem.at[4])
    for copy in (get_w, get_x, get_rules, get_counts, get_cot):
        copy.start()
    barrier = pltpu.get_barrier_semaphore()

    def greet(device):
        pl.semaphore_signal(barrier, inc=1, device_id=device, device_id_type=MESH)

    for d in (*range(1, REACH + 1), *range(NZ - REACH, NZ)):
        greet(at_z(d))
    for d in range(1, NY):
        greet(at_y(d))
    for d in range(1, NX):
        greet(at_x(d))
    for device in (sib, up, down):
        greet(device)
    get_w.wait()
    wz[0, 0:4, :] = win[:, 0:128].astype(F32)
    wz[0, 4:8, :] = win[:, 128:256].astype(F32)
    pl.semaphore_wait(barrier, 2 * REACH + 1 + NY + NX)

    def z_copy(d):
        return remote(wz.at[0], wz.at[d], z_sem, d, at_z(d))

    def each_z(act):
        pl.loop(1, NZ)(act)

    def z_pass(forward):
        if forward:
            src, dst, d = pl.ds(1, REACH), pl.ds(REACH + 1, REACH), REACH
        else:
            src, dst, d = pl.ds(NZ - REACH + 1, REACH - 1), pl.ds(NZ - 2 * REACH + 1, REACH - 1), NZ - REACH
        return remote(wz.at[src], wz.at[dst], z_sem, NZ + int(forward), at_z(d))

    for d in range(REACH, 0, -1):
        send(z_copy(d))
        send(z_copy(NZ - d))

    own_low, own_high = pl.ds(BND, BND), pl.ds(OUT_BLK, BND)
    top, bottom = pl.ds(BND + OUT_BLK, BND), pl.ds(0, BND)
    get_cot.wait()
    send(remote(cot.at[own_low], cot.at[top], h_sem, 0, down))
    send(remote(cot.at[own_high], cot.at[bottom], h_sem, 1, up))

    get_x.wait()
    rows = lax.broadcasted_iota(jnp.int32, (ci, ci), 0)
    cols = lax.broadcasted_iota(jnp.int32, (ci, ci), 1)

    def channel(p):
        from_y = lax.rem(y + NY - lax.div(p, 4 * NZ), NY)
        from_z = lax.rem(z + NZ - lax.div(lax.rem(p, 4 * NZ), 4), NZ)
        return from_z * (4 * NY) + from_y * 4 + lax.rem(p, 4)

    perm = jnp.where(rows == channel(cols), 1.0, 0.0).astype(BF16)
    perm_t = jnp.where(cols == channel(rows), 1.0, 0.0).astype(BF16)

    @pl.loop(0, IN_BLK)
    def _(i):
        block = xin[0, pl.ds(pl.multiple_of(i * br, br), br), :]
        xp[i] = dot(block, perm, NN).astype(BF16)
        xt[i] = dot(perm_t, block, NT).astype(BF16)

    sums[NONE] = jnp.zeros(sums.shape[1:], F32)
    gext[EXT] = jnp.zeros(gext.shape[1:], BF16)

    def kernel_at(t):
        pair = t // 2
        off = pair + (pair // 2) * (1 - 2 * (pair % 2))
        return lax.rem(x + off, NX) * 2 + lax.rem(c + t % 2, 2)

    def chain(t, carry):
        f_last, b_last = list(carry[:EXT]), list(carry[EXT:])
        k = kernel_at(t)
        count = counts[0, k]
        for j in range(SLOTS):
            n = t * SLOTS + j
            source, block, owner = rules[0, 0, k, j], rules[0, 1, k, j], rules[0, 2, k, j]
            slot = BND + block + (owner - space) * OUT_BLK
            live = j < count
            slot = jnp.where(live, slot, EXT)
            start = jnp.where(live, source, IN_BLK)
            f_in[n] = source
            b_slot[n] = slot
            prev = jnp.int32(NONE)
            for o in range(EXT):
                hit = slot == o
                prev = jnp.where(hit, f_last[o], prev)
                f_last[o] = jnp.where(hit, n, f_last[o])
            f_prev[n] = prev
            prev = jnp.int32(NONE)
            for o in range(IN_BLK):
                hit = start == o
                prev = jnp.where(hit, b_last[o], prev)
                b_last[o] = jnp.where(hit, n, b_last[o])
            b_prev[n] = prev
        return tuple(f_last + b_last)

    get_rules.wait()
    get_counts.wait()
    ends = lax.fori_loop(0, OFFS, chain, (jnp.int32(NONE),) * (EXT + IN_BLK))
    for o in range(EXT + IN_BLK):
        lasts[o] = ends[o]

    for d in range(1, REACH + 1):
        z_copy(d).wait_recv()
    send(z_pass(True))
    for d in range(NZ - 1, NZ - REACH - 1, -1):
        z_copy(d).wait_recv()
    if REACH > 1:
        send(z_pass(False))
        z_pass(False).wait_recv()
    z_pass(True).wait_recv()

    low = lax.broadcasted_iota(jnp.int32, (8, 128), 0) < 4
    for p in range(NZ // 2):
        a, b = wz[2 * p], wz[2 * p + 1]
        wst[8 * p : 8 * p + 8, 0:128] = jnp.where(low, a, pltpu.roll(b, 4, 0))
        wst[8 * p : 8 * p + 8, 128:256] = jnp.where(low, pltpu.roll(a, 4, 0), b)
    part = 4 * NZ
    wf[0, 0:part, :] = wst[...].astype(BF16)

    def y_copy(d):
        return remote(wf.at[0, pl.ds(0, part)], wf.at[0, pl.ds(d * part, part)], y_sem, d, at_y(d))

    for d in range(1, NY):
        send(y_copy(d))
    for d in range(1, NY):
        y_copy(d).wait_recv()

    order = (0, 1, 3, 2)

    def x_copy(d):
        return remote(wf.at[0], wf.at[2 * order.index(NX - d)], x_sem, d, at_x(d))

    def c_copy(off):
        t = 2 * order.index(off)
        return remote(wf.at[t], wf.at[t + 1], c_sem, off, sib)

    for d in (1, 3, 2):
        send(x_copy(d))
    send(c_copy(0))

    def arrive(off, other):
        if other:
            c_copy(off).wait_recv()
        elif off:
            x_copy(NX - off).wait_recv()
            send(c_copy(off))

    for t in range(OFFS):
        arrive(order[t // 2], t % 2 == 1)
        flat = xp[...].reshape(IN_BLK * br, ci)
        yb[...] = dot(flat, wf[t], NN).reshape(yb.shape)
        for j in range(SLOTS):
            n = t * SLOTS + j
            sums[n] = yb[f_in[n]] + sums[f_prev[n]]

    for i in range(EXT):
        hs[i] = sums[lasts[i]].astype(BF16)

    def rim_copy(half, upward):
        src = (OUT_BLK if upward else 0) + BND * half
        dst = src - OUT_BLK if upward else src + OUT_BLK
        index = 2 + 2 * int(upward) + half
        return remote(hs.at[pl.ds(src, BND)], hr.at[pl.ds(dst, BND)], h_sem, index, up if upward else down)

    for half in (0, 1):
        send(rim_copy(half, False))
        send(rim_copy(half, True))
    remote(cot.at[own_low], cot.at[top], h_sem, 0, down).wait_recv()
    remote(cot.at[own_high], cot.at[bottom], h_sem, 1, up).wait_recv()
    for half in (0, 1):
        for upward in (True, False):
            rim_copy(half, upward).wait_recv()
            first = (0 if upward else OUT_BLK) + BND * half
            for o in range(first, first + BND):
                pre = sums[lasts[o]] + hr[o].astype(F32)
                sigma = jax.nn.sigmoid(pre)
                if BND <= o < BND + OUT_BLK:
                    act_ref[0, (o - BND) * br : (o - BND + 1) * br, :] = (pre * sigma).astype(BF16)
                upstream = cot[o].astype(F32)
                gext[o] = (upstream * sigma * (1.0 + pre * (1.0 - sigma))).astype(BF16)
    put(act_ref, act_hbm, 5)

    def term(off, other):
        t = 2 * order.index(off) + int(other)
        lhs = [xt[f_in[t * SLOTS + j]] for j in range(SLOTS)]
        rhs = [gext[b_slot[t * SLOTS + j]] for j in range(SLOTS)]
        return dot(jnp.concatenate(lhs, axis=1), jnp.concatenate(rhs, axis=0), NN)

    def to_sibling(off):
        sb_send[off] = term(off, True)
        send(remote(sb_send.at[off], sb_recv.at[off], rc_sem, off, sib))

    sequence = (2, 1, 3, 0)
    to_sibling(sequence[0])
    for i, off in enumerate(sequence):
        own[...] = term(off, False)
        if i + 1 < NX:
            to_sibling(sequence[i + 1])
        remote(sb_send.at[off], sb_recv.at[off], rc_sem, off, sib).wait_recv()
        if off:
            xs[off] = (own[...] + sb_recv[off]).astype(BF16)
            send(remote(xs.at[off], xr.at[off], rx_sem, off, at_x(off)))
        else:
            own[...] += sb_recv[off]

    for t in range(OFFS):
        flat = gext[0:EXT].reshape(EXT * br, gext.shape[2])
        yb[:, :, 0:ci] = dot(flat, wf[t], NT).reshape(EXT, br, ci)
        for j in range(SLOTS):
            n = t * SLOTS + j
            place = jnp.minimum(b_slot[n], EXT - 1)
            sums[n] = yb[place] + sums[b_prev[n]]

    for d in range(1, NX):
        remote(xs.at[d], xr.at[d], rx_sem, d, at_x(d)).wait_recv()
    total = own[...]
    for d in range(1, NX):
        total = total + xr[d].astype(F32)
    own[...] = total
    for d in range(1, NY):
        ys[d] = own[(NY - d) * part : (NY - d + 1) * part, :].astype(BF16)
        send(remote(ys.at[d], yr.at[d], ry_sem, d, at_y(d)))

    for i in range(IN_BLK):
        back = sums[lasts[EXT + i]][:, 0:ci].astype(BF16)
        gf_ref[0, i * br : (i + 1) * br, :] = dot(back, perm_t, NN).astype(BF16)

    put(gf_ref, gf_hbm, 6)

    for d in range(1, NY):
        remote(ys.at[d], yr.at[d], ry_sem, d, at_y(d)).wait_recv()
    total = own[0:part, :]
    for d in range(1, NY):
        total = total + yr[d].astype(F32)
    for p in range(NZ // 2):
        a, b = total[8 * p : 8 * p + 8, 0:128], total[8 * p : 8 * p + 8, 128:256]
        zs[2 * p] = jnp.where(low, a, pltpu.roll(b, 4, 0))
        zs[2 * p + 1] = jnp.where(low, pltpu.roll(a, 4, 0), b)

    def out_copy(d):
        return remote(zs.at[NZ - d], zr.at[d], rz_sem, d, at_z(d))

    each_z(lambda d: out_copy(d).start())
    pending.append(lambda: each_z(lambda d: out_copy(d).wait_send()))
    each_z(lambda d: out_copy(d).wait_recv())

    total = zs[0]
    for d in range(1, NZ):
        total = total + zr[d]
    total = total * grad_scale
    gw_ref[:, 0:128] = total[0:4]
    gw_ref[:, 128:256] = total[4:8]

    put(gw_ref, gw_hbm, 7)
    for wait in pending:
        wait()


def local(features, weight, rulebook, rule_counts, cotangent):
    ci, co = features.shape[2], weight.shape[1]
    br = features.shape[1] // IN_BLK
    hbm = pl.BlockSpec(memory_space=pl.ANY)
    rules = jnp.transpose(rulebook, (0, 2, 1, 3))
    dma = pltpu.SemaphoreType.DMA
    V = pltpu.VMEM
    return pl.pallas_call(
        kernel,
        out_shape=(
            jax.ShapeDtypeStruct(cotangent.shape, BF16),
            jax.ShapeDtypeStruct(features.shape, BF16),
            jax.ShapeDtypeStruct(weight.shape, F32),
        ),
        in_specs=[hbm] * 5,
        out_specs=(hbm, hbm, hbm),
        scratch_shapes=[
            V(features.shape, BF16),
            V(weight.shape, BF16),
            pltpu.SMEM(rules.shape, jnp.int32),
            pltpu.SMEM(rule_counts.shape, jnp.int32),
            V((IN_BLK, br, ci), BF16),
            V((IN_BLK, ci, br), BF16),
            V((EXT, br, co), BF16),
            V((NZ, 8, 128), F32),
            V((4 * NZ, co), F32),
            V((OFFS, ci, co), BF16),
            V((IN_BLK, br, max(ci, co)), F32),
            V((NONE + 1, br, max(ci, co)), F32),
            V((EXT, br, co), BF16),
            V((EXT, br, co), BF16),
            V((EXT + 1, br, co), BF16),
            V(cotangent.shape, BF16),
            V(features.shape, BF16),
            V(weight.shape, F32),
            V((NX, ci, co), F32),
            V((NX, ci, co), F32),
            V((ci, co), F32),
            V((NX, ci, co), BF16),
            V((NX, ci, co), BF16),
            V((NY, 4 * NZ, co), BF16),
            V((NY, 4 * NZ, co), BF16),
            V((NZ, 8, 128), F32),
            V((NZ, 8, 128), F32),
            pltpu.SMEM((NONE,), jnp.int32),
            pltpu.SMEM((NONE,), jnp.int32),
            pltpu.SMEM((NONE,), jnp.int32),
            pltpu.SMEM((NONE,), jnp.int32),
            pltpu.SMEM((EXT + IN_BLK,), jnp.int32),
            dma((8,)),
            dma((2, NZ + 2)),
            dma((2, NY)),
            dma((2, NX)),
            dma((2, NX)),
            dma((2, 6)),
            dma((2, NX)),
            dma((2, NX)),
            dma((2, NY)),
            dma((2, NZ)),
        ],
        compiler_params=pltpu.CompilerParams(
            collective_id=0, has_side_effects=True, vmem_limit_bytes=60 * 1024 * 1024
        ),
    )(features, weight, rules, rule_counts, cotangent.reshape(1, OUT_BLK, br, co))


def solution(mesh):
    in_specs = (
        P("dp", "space", None),
        P(("dp", "space"), None),
        P("dp", "space", None, None),
        P("dp", "space"),
        P("dp", "space", None),
    )
    out_specs = (P("dp", "space", None), P("dp", "space", None), P(("dp", "space"), None))
    return jax.shard_map(local, mesh=mesh, in_specs=in_specs, out_specs=out_specs, check_vma=False)
```

```python
import functools

import jax
import jax.numpy as jnp
from jax import lax
from jax.experimental import pallas as pl
from jax.experimental.pallas import tpu as pltpu
from jax.sharding import PartitionSpec as P

OFFS = 8
BND = 2
SLOTS = 8
IN_BLK = 8
OUT_BLK = 4
EXT = OUT_BLK + 2 * BND
NONE = OFFS * SLOTS

grad_scale = 1.0 / 2048.0
BF16 = jnp.bfloat16
F32 = jnp.float32
MESH = pl.DeviceIdType.MESH

NX, NY, NZ = 4, 4, 16
REACH = 4


def dot(a, b, dims):
    return lax.dot_general(a, b, (dims, ((), ())), preferred_element_type=F32)


NN = ((1,), (0,))
NT = ((1,), (1,))


def kernel(
    feat_hbm, w_hbm, rules_hbm, counts_hbm, cot_hbm,
    act_hbm, gf_hbm, gw_hbm,
    xin, win, rules, counts, xp, xt, cot, wz, wst, wf, yb, sums, hs, hr, gext, act_ref, gf_ref, gw_ref,
    sb_send, sb_recv, own, xs, xr, zs, zr,
    f_in, f_prev, b_slot, b_prev, lasts,
    loc_sem, z_sem, xy_sem, c_sem, h_sem, rc_sem, rx_sem, rz_sem,
):
    ci = xin.shape[2]
    br = xp.shape[1]
    dp = lax.axis_index("dp")
    space = lax.axis_index("space")
    x, c = lax.div(dp, 2), lax.rem(dp, 2)
    z, y = lax.div(space, NY), lax.rem(space, NY)
    oc = 1 - c
    n_space = NY * NZ
    sib = (x * 2 + oc, space)
    up = (dp, lax.rem(space + 1, n_space))
    down = (dp, lax.rem(space + n_space - 1, n_space))

    def x_of(off):
        return lax.rem(x + off, NX)

    def at_xy(dx, dy):
        return (x_of(dx) * 2 + c, z * NY + lax.rem(y + dy, NY))

    def at_z(off):
        return (dp, lax.rem(z + off, NZ) * NY + y)

    def remote(src, dst, sems, index, device):
        return pltpu.make_async_remote_copy(
            src_ref=src, dst_ref=dst, send_sem=sems.at[0, index], recv_sem=sems.at[1, index],
            device_id=device, device_id_type=MESH,
        )

    plane = [(dx, dy) for dx in (0, 1, 3, 2) for dy in range(NY) if dx or dy]
    pending = []

    def send(copy):
        copy.start()
        pending.append(copy.wait_send)

    def put(src, dst, index):
        copy = pltpu.make_async_copy(src, dst, loc_sem.at[index])
        copy.start()
        pending.append(copy.wait)

    get_w = pltpu.make_async_copy(w_hbm, win, loc_sem.at[0])
    get_x = pltpu.make_async_copy(feat_hbm, xin, loc_sem.at[1])
    get_rules = pltpu.make_async_copy(rules_hbm, rules, loc_sem.at[2])
    get_counts = pltpu.make_async_copy(counts_hbm, counts, loc_sem.at[3])
    get_cot = pltpu.make_async_copy(cot_hbm.at[0], cot.at[pl.ds(BND, OUT_BLK)], loc_sem.at[4])
    for copy in (get_w, get_x, get_rules, get_counts, get_cot):
        copy.start()
    barrier = pltpu.get_barrier_semaphore()

    def greet(device):
        pl.semaphore_signal(barrier, inc=1, device_id=device, device_id_type=MESH)

    for d in range(REACH, 0, -1):
        greet(at_z(d))
        greet(at_z(NZ - d))
    for dx, dy in plane:
        greet(at_xy(dx, dy))
    for device in (sib, up, down):
        greet(device)
    get_w.wait()
    wz[0, 0:4, :] = win[:, 0:128].astype(F32)
    wz[0, 4:8, :] = win[:, 128:256].astype(F32)
    pl.semaphore_wait(barrier, 2 * REACH + len(plane) + 3)

    def z_copy(d):
        slot = REACH - 1 + d if d > 0 else -d
        return remote(wz.at[0], wz.at[slot], z_sem, slot, at_z(d % NZ))

    def z_pass(above):
        src, dst = pl.ds(0 if above else REACH, REACH), pl.ds((3 if above else 2) * REACH, REACH)
        return remote(wz.at[src], wz.at[dst], z_sem, NZ + int(above), at_z(NZ - REACH if above else REACH))

    near = [d for far in range(REACH, 0, -1) for d in (far, -far) if d > -REACH]
    for d in near:
        send(z_copy(d))

    own_low, own_high = pl.ds(BND, BND), pl.ds(OUT_BLK, BND)
    top, bottom = pl.ds(BND + OUT_BLK, BND), pl.ds(0, BND)
    get_cot.wait()
    send(remote(cot.at[own_low], cot.at[top], h_sem, 0, down))
    send(remote(cot.at[own_high], cot.at[bottom], h_sem, 1, up))

    get_x.wait()
    rows = lax.broadcasted_iota(jnp.int32, (ci, ci), 0)
    cols = lax.broadcasted_iota(jnp.int32, (ci, ci), 1)

    def channel(p):
        from_y = lax.rem(y + NY - lax.div(p, 4 * NZ), NY)
        tile = lax.div(lax.rem(p, 4 * NZ), 4)
        up_by = jnp.where(tile < REACH, tile, jnp.where(tile < 3 * REACH, REACH - 1 - tile, tile - 2 * REACH))
        from_z = lax.rem(z + NZ + up_by, NZ)
        return from_z * (4 * NY) + from_y * 4 + lax.rem(p, 4)

    perm = jnp.where(rows == channel(cols), 1.0, 0.0).astype(BF16)
    perm_t = jnp.where(cols == channel(rows), 1.0, 0.0).astype(BF16)

    @pl.loop(0, IN_BLK)
    def _(i):
        block = xin[0, pl.ds(pl.multiple_of(i * br, br), br), :]
        xp[i] = dot(block, perm, NN).astype(BF16)
        xt[i] = dot(perm_t, block, NT).astype(BF16)

    sums[NONE] = jnp.zeros(sums.shape[1:], F32)
    gext[EXT] = jnp.zeros(gext.shape[1:], BF16)

    low = lax.broadcasted_iota(jnp.int32, (8, 128), 0) < 4
    part = 4 * NZ

    def unpack(half):
        for p in range(half * NZ // 4, (half + 1) * NZ // 4):
            a, b = wz[2 * p], wz[2 * p + 1]
            wst[8 * p : 8 * p + 8, 0:128] = jnp.where(low, a, pltpu.roll(b, 4, 0))
            wst[8 * p : 8 * p + 8, 128:256] = jnp.where(low, pltpu.roll(a, 4, 0), b)
        rows = slice(half * part // 2, (half + 1) * part // 2)
        wf[0, rows, :] = wst[rows, :].astype(BF16)

    order = (0, 1, 3, 2)

    def xy_copy(half, dx, dy):
        start = half * part // 2
        dst = wf.at[2 * order.index((NX - dx) % NX), pl.ds(dy * part + start, part // 2)]
        index = (half * NX + dx) * NY + dy
        return remote(wf.at[0, pl.ds(start, part // 2)], dst, xy_sem, index, at_xy(dx, dy))

    def c_copy(off):
        t = 2 * order.index(off)
        return remote(wf.at[t], wf.at[t + 1], c_sem, off, sib)

    for d in near:
        z_copy(d).wait_recv()
    send(z_pass(False))
    send(z_pass(True))
    unpack(0)
    for dx, dy in plane:
        send(xy_copy(0, dx, dy))

    def kernel_at(t):
        pair = t // 2
        off = pair + (pair // 2) * (1 - 2 * (pair % 2))
        return lax.rem(x + off, NX) * 2 + lax.rem(c + t % 2, 2)

    def chain(t, carry):
        f_last, b_last = list(carry[:EXT]), list(carry[EXT:])
        k = kernel_at(t)
        count = counts[0, k]
        for j in range(SLOTS):
            n = t * SLOTS + j
            source, block, owner = rules[0, 0, k, j], rules[0, 1, k, j], rules[0, 2, k, j]
            slot = BND + block + (owner - space) * OUT_BLK
            live = j < count
            slot = jnp.where(live, slot, EXT)
            start = jnp.where(live, source, IN_BLK)
            f_in[n] = source
            b_slot[n] = slot
            prev = jnp.int32(NONE)
            for o in range(EXT):
                hit = slot == o
                prev = jnp.where(hit, f_last[o], prev)
                f_last[o] = jnp.where(hit, n, f_last[o])
            f_prev[n] = prev
            prev = jnp.int32(NONE)
            for o in range(IN_BLK):
                hit = start == o
                prev = jnp.where(hit, b_last[o], prev)
                b_last[o] = jnp.where(hit, n, b_last[o])
            b_prev[n] = prev
        return tuple(f_last + b_last)

    get_rules.wait()
    get_counts.wait()
    ends = lax.fori_loop(0, OFFS, chain, (jnp.int32(NONE),) * (EXT + IN_BLK))
    for o in range(EXT + IN_BLK):
        lasts[o] = ends[o]

    z_pass(False).wait_recv()
    z_pass(True).wait_recv()
    unpack(1)
    for dx, dy in plane:
        send(xy_copy(1, dx, dy))

    def arrive(off, other):
        if other:
            c_copy(off).wait_recv()
        else:
            for dy in range(NY):
                if off or dy:
                    xy_copy(0, (NX - off) % NX, dy).wait_recv()
                    xy_copy(1, (NX - off) % NX, dy).wait_recv()
            send(c_copy(off))

    for t in range(OFFS):
        arrive(order[t // 2], t % 2 == 1)
        flat = xp[...].reshape(IN_BLK * br, ci)
        yb[...] = dot(flat, wf[t], NN).reshape(yb.shape)
        for j in range(SLOTS):
            n = t * SLOTS + j
            sums[n] = yb[f_in[n]] + sums[f_prev[n]]

    def rim_copy(i, upward):
        src, dst = (i + OUT_BLK, i) if upward else (i, i + OUT_BLK)
        index = 2 + OUT_BLK * int(upward) + i
        return remote(hs.at[src], hr.at[dst], h_sem, index, up if upward else down)

    for i in range(OUT_BLK):
        for upward in (False, True):
            o = i + OUT_BLK * int(upward)
            hs[o] = sums[lasts[o]].astype(BF16)
            send(rim_copy(i, upward))
    remote(cot.at[own_low], cot.at[top], h_sem, 0, down).wait_recv()
    remote(cot.at[own_high], cot.at[bottom], h_sem, 1, up).wait_recv()
    for i in range(OUT_BLK):
        for upward in (False, True):
            rim_copy(i, upward).wait_recv()
            o = i + (0 if upward else OUT_BLK)
            pre = sums[lasts[o]] + hr[o].astype(F32)
            sigma = jax.nn.sigmoid(pre)
            if BND <= o < BND + OUT_BLK:
                act_ref[0, (o - BND) * br : (o - BND + 1) * br, :] = (pre * sigma).astype(BF16)
            upstream = cot[o].astype(F32)
            gext[o] = (upstream * sigma * (1.0 + pre * (1.0 - sigma))).astype(BF16)
    put(act_ref, act_hbm, 5)

    def term(off, other):
        t = 2 * order.index(off) + int(other)
        lhs = [xt[f_in[t * SLOTS + j]] for j in range(SLOTS)]
        rhs = [gext[b_slot[t * SLOTS + j]] for j in range(SLOTS)]
        return dot(jnp.concatenate(lhs, axis=1), jnp.concatenate(rhs, axis=0), NN)

    def to_sibling(off):
        sb_send[off] = term(off, True)
        send(remote(sb_send.at[off], sb_recv.at[off], rc_sem, off, sib))

    def part_copy(dx, dy):
        src = xs.at[dx, pl.ds((NY - dy) % NY * part, part)]
        return remote(src, xr.at[dx * NY + dy], rx_sem, dx * NY + dy, at_xy(dx, dy))

    sequence = (2, 1, 3, 0)
    to_sibling(sequence[0])
    for i, off in enumerate(sequence):
        own[...] = term(off, False)
        if i + 1 < NX:
            to_sibling(sequence[i + 1])
        remote(sb_send.at[off], sb_recv.at[off], rc_sem, off, sib).wait_recv()
        own[...] += sb_recv[off]
        xs[off] = own[...].astype(BF16)
        for dy in sorted(range(NY), key=lambda d: -min(d, NY - d)):
            if off or dy:
                send(part_copy(off, dy))

    for t in range(OFFS):
        flat = gext[0:EXT].reshape(EXT * br, gext.shape[2])
        yb[:, :, 0:ci] = dot(flat, wf[t], NT).reshape(EXT, br, ci)
        for j in range(SLOTS):
            n = t * SLOTS + j
            place = jnp.minimum(b_slot[n], EXT - 1)
            sums[n] = yb[place] + sums[b_prev[n]]

    for i in range(IN_BLK):
        back = sums[lasts[EXT + i]][:, 0:ci].astype(BF16)
        gf_ref[0, i * br : (i + 1) * br, :] = dot(back, perm_t, NN).astype(BF16)

    put(gf_ref, gf_hbm, 6)

    total = own[0:part, :]
    for dx, dy in plane:
        part_copy(dx, dy).wait_recv()
    for dx, dy in plane:
        total = total + xr[dx * NY + dy].astype(F32)
    for p in range(NZ // 2):
        a, b = total[8 * p : 8 * p + 8, 0:128], total[8 * p : 8 * p + 8, 128:256]
        zs[2 * p] = jnp.where(low, a, pltpu.roll(b, 4, 0))
        zs[2 * p + 1] = jnp.where(low, pltpu.roll(a, 4, 0), b)

    def out_copy(d):
        if d < 2 * REACH:
            tile = d if d < REACH else d + 2 * REACH
        else:
            tile = REACH - 1 + NZ - d
        return remote(zs.at[tile], zr.at[d], rz_sem, d, at_z(d))

    far_first = sorted(range(1, NZ), key=lambda d: -min(d, NZ - d))
    for d in far_first:
        send(out_copy(d))
    for d in range(1, NZ):
        out_copy(d).wait_recv()

    total = zs[0]
    for d in range(1, NZ):
        total = total + zr[d]
    total = total * grad_scale
    gw_ref[:, 0:128] = total[0:4]
    gw_ref[:, 128:256] = total[4:8]

    put(gw_ref, gw_hbm, 7)
    for wait in pending:
        wait()


def local(features, weight, rulebook, rule_counts, cotangent):
    ci, co = features.shape[2], weight.shape[1]
    br = features.shape[1] // IN_BLK
    hbm = pl.BlockSpec(memory_space=pl.ANY)
    rules = jnp.transpose(rulebook, (0, 2, 1, 3))
    dma = pltpu.SemaphoreType.DMA
    V = pltpu.VMEM
    return pl.pallas_call(
        kernel,
        out_shape=(
            jax.ShapeDtypeStruct(cotangent.shape, BF16),
            jax.ShapeDtypeStruct(features.shape, BF16),
            jax.ShapeDtypeStruct(weight.shape, F32),
        ),
        in_specs=[hbm] * 5,
        out_specs=(hbm, hbm, hbm),
        scratch_shapes=[
            V(features.shape, BF16),
            V(weight.shape, BF16),
            pltpu.SMEM(rules.shape, jnp.int32),
            pltpu.SMEM(rule_counts.shape, jnp.int32),
            V((IN_BLK, br, ci), BF16),
            V((IN_BLK, ci, br), BF16),
            V((EXT, br, co), BF16),
            V((NZ, 8, 128), F32),
            V((4 * NZ, co), F32),
            V((OFFS, ci, co), BF16),
            V((IN_BLK, br, max(ci, co)), F32),
            V((NONE + 1, br, max(ci, co)), F32),
            V((EXT, br, co), BF16),
            V((EXT, br, co), BF16),
            V((EXT + 1, br, co), BF16),
            V(cotangent.shape, BF16),
            V(features.shape, BF16),
            V(weight.shape, F32),
            V((NX, ci, co), F32),
            V((NX, ci, co), F32),
            V((ci, co), F32),
            V((NX, ci, co), BF16),
            V((NX * NY, 4 * NZ, co), BF16),
            V((NZ, 8, 128), F32),
            V((NZ, 8, 128), F32),
            pltpu.SMEM((NONE,), jnp.int32),
            pltpu.SMEM((NONE,), jnp.int32),
            pltpu.SMEM((NONE,), jnp.int32),
            pltpu.SMEM((NONE,), jnp.int32),
            pltpu.SMEM((EXT + IN_BLK,), jnp.int32),
            dma((8,)),
            dma((2, NZ + 2)),
            dma((2, 2 * NX * NY)),
            dma((2, NX)),
            dma((2, 2 + 2 * OUT_BLK)),
            dma((2, NX)),
            dma((2, NX * NY)),
            dma((2, NZ)),
        ],
        compiler_params=pltpu.CompilerParams(
            collective_id=0, has_side_effects=True, vmem_limit_bytes=60 * 1024 * 1024
        ),
    )(features, weight, rules, rule_counts, cotangent.reshape(1, OUT_BLK, br, co))


def solution(mesh):
    in_specs = (
        P("dp", "space", None),
        P(("dp", "space"), None),
        P("dp", "space", None, None),
        P("dp", "space"),
        P("dp", "space", None),
    )
    out_specs = (P("dp", "space", None), P("dp", "space", None), P(("dp", "space"), None))
    return jax.shard_map(local, mesh=mesh, in_specs=in_specs, out_specs=out_specs, check_vma=False)
```

```python
import jax
import jax.numpy as jnp
from jax import lax
from jax.experimental import pallas as pl
from jax.experimental.pallas import tpu as pltpu
from jax.sharding import PartitionSpec as P

OFFS = 8
BND = 2
SLOTS = 8
IN_BLK = 8
OUT_BLK = 4
EXT = OUT_BLK + 2 * BND
NONE = OFFS * SLOTS

grad_scale = 1.0 / 2048.0
BF16 = jnp.bfloat16
F32 = jnp.float32
MESH = pl.DeviceIdType.MESH

NX, NY, NZ = 4, 4, 16
REACH = 4


def dot(a, b, dims):
    return lax.dot_general(a, b, (dims, ((), ())), preferred_element_type=F32)


NN = ((1,), (0,))
NT = ((1,), (1,))


def kernel(
    feat_hbm, w_hbm, rules_hbm, counts_hbm, cot_hbm,
    act_hbm, gf_hbm, gw_hbm,
    xin, win, rules, counts, xp, xt, cot, wz, wst, wf, sums, hs, hr, gext, act_ref, gf_ref, gw_ref,
    sb_send, sb_recv, own, xs, xr, zs, zr,
    f_in, f_prev, b_slot, b_prev, lasts,
    loc_sem, z_sem, xy_sem, c_sem, h_sem, rc_sem, rx_sem, rz_sem,
):
    ci = xin.shape[2]
    br, co = xp.shape[1], wf.shape[2]
    dp = lax.axis_index("dp")
    space = lax.axis_index("space")
    x, c = lax.div(dp, 2), lax.rem(dp, 2)
    z, y = lax.div(space, NY), lax.rem(space, NY)
    oc = 1 - c
    n_space = NY * NZ
    sib = (x * 2 + oc, space)
    up = (dp, lax.rem(space + 1, n_space))
    down = (dp, lax.rem(space + n_space - 1, n_space))

    def x_of(off):
        return lax.rem(x + off, NX)

    def at_xy(dx, dy):
        return (x_of(dx) * 2 + c, z * NY + lax.rem(y + dy, NY))

    def at_z(off):
        return (dp, lax.rem(z + off, NZ) * NY + y)

    def remote(src, dst, sems, index, device):
        return pltpu.make_async_remote_copy(
            src_ref=src, dst_ref=dst, send_sem=sems.at[0, index], recv_sem=sems.at[1, index],
            device_id=device, device_id_type=MESH,
        )

    plane = [(dx, dy) for dx in (0, 1, 3, 2) for dy in (2, 1, 3, 0) if dx or dy]
    pending = []

    def send(copy):
        copy.start()
        pending.append(copy.wait_send)

    def put(src, dst, index):
        copy = pltpu.make_async_copy(src, dst, loc_sem.at[index])
        copy.start()
        pending.append(copy.wait)

    get_w = pltpu.make_async_copy(w_hbm, win, loc_sem.at[0])
    get_x = pltpu.make_async_copy(feat_hbm, xin, loc_sem.at[1])
    get_rules = pltpu.make_async_copy(rules_hbm, rules, loc_sem.at[2])
    get_counts = pltpu.make_async_copy(counts_hbm, counts, loc_sem.at[3])
    get_cot = pltpu.make_async_copy(cot_hbm.at[0], cot.at[pl.ds(BND, OUT_BLK)], loc_sem.at[4])
    for copy in (get_w, get_x, get_rules, get_counts, get_cot):
        copy.start()
    barrier = pltpu.get_barrier_semaphore()

    def greet(device):
        pl.semaphore_signal(barrier, inc=1, device_id=device, device_id_type=MESH)

    for d in range(REACH, 0, -1):
        greet(at_z(d))
        greet(at_z(NZ - d))
    for dx, dy in plane:
        greet(at_xy(dx, dy))
    for device in (sib, up, down):
        greet(device)
    get_w.wait()
    wz[0, 0:4, :] = win[:, 0:128].astype(F32)
    wz[0, 4:8, :] = win[:, 128:256].astype(F32)
    pl.semaphore_wait(barrier, 2 * REACH + len(plane) + 3)

    def z_copy(d):
        slot = REACH - 1 + d if d > 0 else -d
        return remote(wz.at[0], wz.at[slot], z_sem, slot, at_z(d % NZ))

    def z_pass(above):
        src, dst = pl.ds(0 if above else REACH, REACH), pl.ds((3 if above else 2) * REACH, REACH)
        return remote(wz.at[src], wz.at[dst], z_sem, NZ + int(above), at_z(NZ - REACH if above else REACH))

    near = [d for far in range(REACH, 0, -1) for d in (far, -far) if d > -REACH]
    for d in near:
        send(z_copy(d))

    get_x.wait()
    rows = lax.broadcasted_iota(jnp.int32, (ci, ci), 0)
    cols = lax.broadcasted_iota(jnp.int32, (ci, ci), 1)

    def channel(p):
        from_y = lax.rem(y + NY - lax.div(p, 4 * NZ), NY)
        tile = lax.div(lax.rem(p, 4 * NZ), 4)
        up_by = jnp.where(tile < REACH, tile, jnp.where(tile < 3 * REACH, REACH - 1 - tile, tile - 2 * REACH))
        from_z = lax.rem(z + NZ + up_by, NZ)
        return from_z * (4 * NY) + from_y * 4 + lax.rem(p, 4)

    perm = jnp.where(rows == channel(cols), 1.0, 0.0).astype(BF16)
    perm_t = jnp.where(cols == channel(rows), 1.0, 0.0).astype(BF16)

    @pl.loop(0, IN_BLK)
    def _(i):
        block = xin[0, pl.ds(pl.multiple_of(i * br, br), br), :]
        xp[i] = dot(block, perm, NN).astype(BF16)
        xt[i] = dot(perm_t, block, NT).astype(BF16)

    sums[NONE] = jnp.zeros(sums.shape[1:], F32)
    gext[EXT] = jnp.zeros(gext.shape[1:], BF16)

    low = lax.broadcasted_iota(jnp.int32, (8, 128), 0) < 4
    part = 4 * NZ

    def unpack(half):
        for p in range(half * NZ // 4, (half + 1) * NZ // 4):
            a, b = wz[2 * p], wz[2 * p + 1]
            wst[8 * p : 8 * p + 8, 0:128] = jnp.where(low, a, pltpu.roll(b, 4, 0))
            wst[8 * p : 8 * p + 8, 128:256] = jnp.where(low, pltpu.roll(a, 4, 0), b)
        rows = slice(half * part // 2, (half + 1) * part // 2)
        wf[0, rows, :] = wst[rows, :].astype(BF16)

    order = (0, 1, 3, 2)

    def xy_copy(half, dx, dy):
        start = half * part // 2
        dst = wf.at[2 * order.index((NX - dx) % NX), pl.ds(dy * part + start, part // 2)]
        index = (half * NX + dx) * NY + dy
        return remote(wf.at[0, pl.ds(start, part // 2)], dst, xy_sem, index, at_xy(dx, dy))

    def c_copy(off):
        t = 2 * order.index(off)
        return remote(wf.at[t], wf.at[t + 1], c_sem, off, sib)

    for d in near:
        z_copy(d).wait_recv()
    send(z_pass(False))
    send(z_pass(True))
    unpack(0)
    for dx, dy in plane:
        send(xy_copy(0, dx, dy))

    def kernel_at(t):
        pair = t // 2
        off = pair + (pair // 2) * (1 - 2 * (pair % 2))
        return lax.rem(x + off, NX) * 2 + lax.rem(c + t % 2, 2)

    def chain(t, carry):
        f_last, b_last = list(carry[:EXT]), list(carry[EXT:])
        k = kernel_at(t)
        count = counts[0, k]
        for j in range(SLOTS):
            n = t * SLOTS + j
            source, block, owner = rules[0, 0, k, j], rules[0, 1, k, j], rules[0, 2, k, j]
            slot = BND + block + (owner - space) * OUT_BLK
            live = j < count
            slot = jnp.where(live, slot, EXT)
            start = jnp.where(live, source, IN_BLK)
            f_in[n] = source
            b_slot[n] = slot
            prev = jnp.int32(NONE)
            for o in range(EXT):
                hit = slot == o
                prev = jnp.where(hit, f_last[o], prev)
                f_last[o] = jnp.where(hit, n, f_last[o])
            f_prev[n] = prev
            prev = jnp.int32(NONE)
            for o in range(IN_BLK):
                hit = start == o
                prev = jnp.where(hit, b_last[o], prev)
                b_last[o] = jnp.where(hit, n, b_last[o])
            b_prev[n] = prev
        return tuple(f_last + b_last)

    get_rules.wait()
    get_counts.wait()
    ends = lax.fori_loop(0, OFFS, chain, (jnp.int32(NONE),) * (EXT + IN_BLK))
    for o in range(EXT + IN_BLK):
        lasts[o] = ends[o]

    z_pass(False).wait_recv()
    z_pass(True).wait_recv()
    unpack(1)
    for dx, dy in plane:
        send(xy_copy(1, dx, dy))

    def arrive(off, other):
        if other:
            c_copy(off).wait_recv()
        else:
            for dy in range(NY):
                if off or dy:
                    xy_copy(0, (NX - off) % NX, dy).wait_recv()
                    xy_copy(1, (NX - off) % NX, dy).wait_recv()
            send(c_copy(off))

    own_low, own_high = pl.ds(BND, BND), pl.ds(OUT_BLK, BND)
    top, bottom = pl.ds(BND + OUT_BLK, BND), pl.ds(0, BND)
    for t in range(OFFS):
        if t == OFFS // 2:
            get_cot.wait()
            send(remote(cot.at[own_low], cot.at[top], h_sem, 0, down))
            send(remote(cot.at[own_high], cot.at[bottom], h_sem, 1, up))
        arrive(order[t // 2], t % 2 == 1)
        picked = [xp[f_in[t * SLOTS + j]] for j in range(SLOTS)]
        products = dot(jnp.concatenate(picked, axis=0), wf[t], NN)
        for j in range(SLOTS):
            n = t * SLOTS + j
            sums[n, :, 0:co] = products[j * br : (j + 1) * br] + sums[f_prev[n]][:, 0:co]

    def rim_copy(i, upward):
        src, dst = (i + OUT_BLK, i) if upward else (i, i + OUT_BLK)
        index = 2 + OUT_BLK * int(upward) + i
        return remote(hs.at[src], hr.at[dst], h_sem, index, up if upward else down)

    for i in range(OUT_BLK):
        for upward in (False, True):
            o = i + OUT_BLK * int(upward)
            hs[o] = sums[lasts[o]].astype(BF16)
            send(rim_copy(i, upward))
    remote(cot.at[own_low], cot.at[top], h_sem, 0, down).wait_recv()
    remote(cot.at[own_high], cot.at[bottom], h_sem, 1, up).wait_recv()
    for i in range(OUT_BLK):
        for upward in (False, True):
            rim_copy(i, upward).wait_recv()
            o = i + (0 if upward else OUT_BLK)
            pre = sums[lasts[o]] + hr[o].astype(F32)
            sigma = jax.nn.sigmoid(pre)
            if BND <= o < BND + OUT_BLK:
                act_ref[0, (o - BND) * br : (o - BND + 1) * br, :] = (pre * sigma).astype(BF16)
            upstream = cot[o].astype(F32)
            gext[o] = (upstream * sigma * (1.0 + pre * (1.0 - sigma))).astype(BF16)
    put(act_ref, act_hbm, 5)

    def term(off, other):
        t = 2 * order.index(off) + int(other)
        lhs = [xt[f_in[t * SLOTS + j]] for j in range(SLOTS)]
        rhs = [gext[b_slot[t * SLOTS + j]] for j in range(SLOTS)]
        return dot(jnp.concatenate(lhs, axis=1), jnp.concatenate(rhs, axis=0), NN)

    def to_sibling(off):
        sb_send[off] = term(off, True)
        send(remote(sb_send.at[off], sb_recv.at[off], rc_sem, off, sib))

    def part_copy(dx, dy):
        src = xs.at[dx, pl.ds((NY - dy) % NY * part, part)]
        return remote(src, xr.at[dx * NY + dy], rx_sem, dx * NY + dy, at_xy(dx, dy))

    sequence = (2, 1, 3, 0)
    to_sibling(sequence[0])
    for i, off in enumerate(sequence):
        own[...] = term(off, False)
        if i + 1 < NX:
            to_sibling(sequence[i + 1])
        remote(sb_send.at[off], sb_recv.at[off], rc_sem, off, sib).wait_recv()
        own[...] += sb_recv[off]
        xs[off] = own[...].astype(BF16)
        for dy in sorted(range(NY), key=lambda d: -min(d, NY - d)):
            if off or dy:
                send(part_copy(off, dy))

    def back(t):
        picked = [gext[b_slot[t * SLOTS + j]] for j in range(SLOTS)]
        products = dot(jnp.concatenate(picked, axis=0), wf[t], NT)
        for j in range(SLOTS):
            n = t * SLOTS + j
            sums[n, :, 0:ci] = products[j * br : (j + 1) * br] + sums[b_prev[n]][:, 0:ci]

    for t in range(OFFS // 2):
        back(t)

    total = own[0:part, :]
    for dx, dy in plane:
        part_copy(dx, dy).wait_recv()
    for dx, dy in plane:
        total = total + xr[dx * NY + dy].astype(F32)
    for p in range(NZ // 2):
        a, b = total[8 * p : 8 * p + 8, 0:128], total[8 * p : 8 * p + 8, 128:256]
        zs[2 * p] = jnp.where(low, a, pltpu.roll(b, 4, 0))
        zs[2 * p + 1] = jnp.where(low, pltpu.roll(a, 4, 0), b)

    def out_copy(d):
        if d < 2 * REACH:
            tile = d if d < REACH else d + 2 * REACH
        else:
            tile = REACH - 1 + NZ - d
        return remote(zs.at[tile], zr.at[d], rz_sem, d, at_z(d))

    far_first = sorted(range(1, NZ), key=lambda d: -min(d, NZ - d))
    for d in far_first:
        send(out_copy(d))

    for t in range(OFFS // 2, OFFS):
        back(t)
    for i in range(IN_BLK):
        ready = sums[lasts[EXT + i]][:, 0:ci].astype(BF16)
        gf_ref[0, i * br : (i + 1) * br, :] = dot(ready, perm_t, NN).astype(BF16)
    put(gf_ref, gf_hbm, 6)
    for wait in pending:
        wait()
    pending.clear()

    for d in range(1, NZ):
        out_copy(d).wait_recv()

    total = zs[0]
    for d in range(1, NZ):
        total = total + zr[d]
    total = total * grad_scale
    gw_ref[:, 0:128] = total[0:4]
    gw_ref[:, 128:256] = total[4:8]

    put(gw_ref, gw_hbm, 7)
    for wait in pending:
        wait()


def hand_over(act, gf, gw, act_out, gf_out, gw_out, act_here, gf_here, gw_here, sems):
    arrays = ((act, act_here, act_out), (gf, gf_here, gf_out), (gw, gw_here, gw_out))
    into = [pltpu.make_async_copy(a, here, sems.at[0, i]) for i, (a, here, _) in enumerate(arrays)]
    out = [pltpu.make_async_copy(here, b, sems.at[1, i]) for i, (_, here, b) in enumerate(arrays)]
    for copy in into:
        copy.start()
    for first, then in zip(into, out):
        first.wait()
        then.start()
    for copy in out:
        copy.wait()


def local(features, weight, rulebook, rule_counts, cotangent):
    ci, co = features.shape[2], weight.shape[1]
    br = features.shape[1] // IN_BLK
    hbm = pl.BlockSpec(memory_space=pl.ANY)
    rules = jnp.transpose(rulebook, (0, 2, 1, 3))
    dma = pltpu.SemaphoreType.DMA
    V = pltpu.VMEM
    results = pl.pallas_call(
        kernel,
        out_shape=(
            jax.ShapeDtypeStruct(cotangent.shape, BF16),
            jax.ShapeDtypeStruct(features.shape, BF16),
            jax.ShapeDtypeStruct(weight.shape, F32),
        ),
        in_specs=[hbm] * 5,
        out_specs=(hbm, hbm, hbm),
        scratch_shapes=[
            V(features.shape, BF16),
            V(weight.shape, BF16),
            pltpu.SMEM(rules.shape, jnp.int32),
            pltpu.SMEM(rule_counts.shape, jnp.int32),
            V((IN_BLK, br, ci), BF16),
            V((IN_BLK, ci, br), BF16),
            V((EXT, br, co), BF16),
            V((NZ, 8, 128), F32),
            V((4 * NZ, co), F32),
            V((OFFS, ci, co), BF16),
            V((NONE + 1, br, max(ci, co)), F32),
            V((EXT, br, co), BF16),
            V((EXT, br, co), BF16),
            V((EXT + 1, br, co), BF16),
            V(cotangent.shape, BF16),
            V(features.shape, BF16),
            V(weight.shape, F32),
            V((NX, ci, co), F32),
            V((NX, ci, co), F32),
            V((ci, co), F32),
            V((NX, ci, co), BF16),
            V((NX * NY, 4 * NZ, co), BF16),
            V((NZ, 8, 128), F32),
            V((NZ, 8, 128), F32),
            pltpu.SMEM((NONE,), jnp.int32),
            pltpu.SMEM((NONE,), jnp.int32),
            pltpu.SMEM((NONE,), jnp.int32),
            pltpu.SMEM((NONE,), jnp.int32),
            pltpu.SMEM((EXT + IN_BLK,), jnp.int32),
            dma((8,)),
            dma((2, NZ + 2)),
            dma((2, 2 * NX * NY)),
            dma((2, NX)),
            dma((2, 2 + 2 * OUT_BLK)),
            dma((2, NX)),
            dma((2, NX * NY)),
            dma((2, NZ)),
        ],
        compiler_params=pltpu.CompilerParams(
            collective_id=0, has_side_effects=True, vmem_limit_bytes=60 * 1024 * 1024
        ),
    )(features, weight, rules, rule_counts, cotangent.reshape(1, OUT_BLK, br, co))
    return pl.pallas_call(
        hand_over,
        out_shape=tuple(jax.ShapeDtypeStruct(r.shape, r.dtype) for r in results),
        in_specs=[hbm] * 3,
        out_specs=(hbm,) * 3,
        scratch_shapes=[V(r.shape, r.dtype) for r in results] + [dma((2, 3))],
        compiler_params=pltpu.CompilerParams(vmem_limit_bytes=60 * 1024 * 1024),
    )(*results)


def solution(mesh):
    in_specs = (
        P("dp", "space", None),
        P(("dp", "space"), None),
        P("dp", "space", None, None),
        P("dp", "space"),
        P("dp", "space", None),
    )
    out_specs = (P("dp", "space", None), P("dp", "space", None), P(("dp", "space"), None))
    return jax.shard_map(local, mesh=mesh, in_specs=in_specs, out_specs=out_specs, check_vma=False)
```

```python
import jax
import jax.numpy as jnp
from jax import lax
from jax.experimental import pallas as pl
from jax.experimental.pallas import tpu as pltpu
from jax.sharding import PartitionSpec as P

OFFS = 8
BND = 2
SLOTS = 8
IN_BLK = 8
OUT_BLK = 4
EXT = OUT_BLK + 2 * BND
NONE = OFFS * SLOTS

grad_scale = 1.0 / 2048.0
BF16 = jnp.bfloat16
F32 = jnp.float32
MESH = pl.DeviceIdType.MESH

NX, NY, NZ = 4, 4, 16
REACH = 4


def dot(a, b, dims):
    return lax.dot_general(a, b, (dims, ((), ())), preferred_element_type=F32)


NN = ((1,), (0,))
NT = ((1,), (1,))


def kernel(
    feat_hbm, w_hbm, rules_hbm, counts_hbm, cot_hbm,
    act_hbm, gf_hbm, gw_hbm,
    xin, win, rules, counts, xp, xt, cot, wz, wst, wf, sums, hs, hr, gext, act_ref, gf_ref, gw_ref,
    sb_send, sb_recv, own, xs, xr, zs, zr,
    f_in, f_prev, b_slot, b_prev, lasts,
    loc_sem, z_sem, xy_sem, c_sem, h_sem, rc_sem, rx_sem, rz_sem,
):
    ci = xin.shape[2]
    br, co = xp.shape[1], wf.shape[2]
    dp = lax.axis_index("dp")
    space = lax.axis_index("space")
    x, c = lax.div(dp, 2), lax.rem(dp, 2)
    z, y = lax.div(space, NY), lax.rem(space, NY)
    oc = 1 - c
    n_space = NY * NZ
    sib = (x * 2 + oc, space)
    up = (dp, lax.rem(space + 1, n_space))
    down = (dp, lax.rem(space + n_space - 1, n_space))

    def x_of(off):
        return lax.rem(x + off, NX)

    def at_xy(dx, dy):
        return (x_of(dx) * 2 + c, z * NY + lax.rem(y + dy, NY))

    def at_z(off):
        return (dp, lax.rem(z + off, NZ) * NY + y)

    def remote(src, dst, sems, index, device):
        return pltpu.make_async_remote_copy(
            src_ref=src, dst_ref=dst, send_sem=sems.at[0, index], recv_sem=sems.at[1, index],
            device_id=device, device_id_type=MESH,
        )

    plane = [(dx, dy) for dx in (0, 1, 3, 2) for dy in (2, 1, 3, 0) if dx or dy]
    pending = []

    def send(copy):
        copy.start()
        pending.append(copy.wait_send)

    def put(src, dst, index):
        copy = pltpu.make_async_copy(src, dst, loc_sem.at[index])
        copy.start()
        pending.append(copy.wait)

    get_w = pltpu.make_async_copy(w_hbm, win, loc_sem.at[0])
    get_x = pltpu.make_async_copy(feat_hbm, xin, loc_sem.at[1])
    get_rules = pltpu.make_async_copy(rules_hbm, rules, loc_sem.at[2])
    get_counts = pltpu.make_async_copy(counts_hbm, counts, loc_sem.at[3])
    get_cot = pltpu.make_async_copy(cot_hbm.at[0], cot.at[pl.ds(BND, OUT_BLK)], loc_sem.at[4])
    for copy in (get_w, get_x, get_rules, get_counts, get_cot):
        copy.start()
    barrier = pltpu.get_barrier_semaphore()

    def greet(device):
        pl.semaphore_signal(barrier, inc=1, device_id=device, device_id_type=MESH)

    for d in range(REACH, 0, -1):
        greet(at_z(d))
        greet(at_z(NZ - d))
    for dx, dy in plane:
        greet(at_xy(dx, dy))
    for device in (sib, up, down):
        greet(device)
    get_w.wait()
    wz[0, 0:4, :] = win[:, 0:128].astype(F32)
    wz[0, 4:8, :] = win[:, 128:256].astype(F32)
    pl.semaphore_wait(barrier, 2 * REACH + len(plane) + 3)

    def z_copy(d):
        slot = REACH - 1 + d if d > 0 else -d
        return remote(wz.at[0], wz.at[slot], z_sem, slot, at_z(d % NZ))

    def z_pass(above):
        src, dst = pl.ds(0 if above else REACH, REACH), pl.ds((3 if above else 2) * REACH, REACH)
        return remote(wz.at[src], wz.at[dst], z_sem, NZ + int(above), at_z(NZ - REACH if above else REACH))

    near = [d for far in range(REACH, 0, -1) for d in (far, -far) if d > -REACH]
    for d in near:
        send(z_copy(d))

    get_x.wait()
    rows = lax.broadcasted_iota(jnp.int32, (ci, ci), 0)
    cols = lax.broadcasted_iota(jnp.int32, (ci, ci), 1)

    def channel(p):
        from_y = lax.rem(y + NY - lax.div(p, 4 * NZ), NY)
        tile = lax.div(lax.rem(p, 4 * NZ), 4)
        up_by = jnp.where(tile < REACH, tile, jnp.where(tile < 3 * REACH, REACH - 1 - tile, tile - 2 * REACH))
        from_z = lax.rem(z + NZ + up_by, NZ)
        return from_z * (4 * NY) + from_y * 4 + lax.rem(p, 4)

    perm = jnp.where(rows == channel(cols), 1.0, 0.0).astype(BF16)
    perm_t = jnp.where(cols == channel(rows), 1.0, 0.0).astype(BF16)

    @pl.loop(0, IN_BLK)
    def _(i):
        block = xin[0, pl.ds(pl.multiple_of(i * br, br), br), :]
        xp[i] = dot(block, perm, NN).astype(BF16)
        xt[i] = dot(perm_t, block, NT).astype(BF16)

    sums[NONE] = jnp.zeros(sums.shape[1:], F32)
    gext[EXT] = jnp.zeros(gext.shape[1:], BF16)

    low = lax.broadcasted_iota(jnp.int32, (8, 128), 0) < 4
    part = 4 * NZ

    def unpack(half):
        for p in range(half * NZ // 4, (half + 1) * NZ // 4):
            a, b = wz[2 * p], wz[2 * p + 1]
            wst[8 * p : 8 * p + 8, 0:128] = jnp.where(low, a, pltpu.roll(b, 4, 0))
            wst[8 * p : 8 * p + 8, 128:256] = jnp.where(low, pltpu.roll(a, 4, 0), b)
        rows = slice(half * part // 2, (half + 1) * part // 2)
        wf[0, rows, :] = wst[rows, :].astype(BF16)

    order = (0, 1, 3, 2)

    def xy_copy(half, dx, dy):
        start = half * part // 2
        dst = wf.at[2 * order.index((NX - dx) % NX), pl.ds(dy * part + start, part // 2)]
        index = (half * NX + dx) * NY + dy
        return remote(wf.at[0, pl.ds(start, part // 2)], dst, xy_sem, index, at_xy(dx, dy))

    def c_copy(off):
        t = 2 * order.index(off)
        return remote(wf.at[t], wf.at[t + 1], c_sem, off, sib)

    for d in near:
        z_copy(d).wait_recv()
    send(z_pass(False))
    send(z_pass(True))
    unpack(0)
    for dx, dy in plane:
        send(xy_copy(0, dx, dy))

    def kernel_at(t):
        pair = t // 2
        off = pair + (pair // 2) * (1 - 2 * (pair % 2))
        return lax.rem(x + off, NX) * 2 + lax.rem(c + t % 2, 2)

    def chain(t, carry):
        f_last, b_last = list(carry[:EXT]), list(carry[EXT:])
        k = kernel_at(t)
        count = counts[0, k]
        for j in range(SLOTS):
            n = t * SLOTS + j
            source, block, owner = rules[0, 0, k, j], rules[0, 1, k, j], rules[0, 2, k, j]
            slot = BND + block + (owner - space) * OUT_BLK
            live = j < count
            slot = jnp.where(live, slot, EXT)
            start = jnp.where(live, source, IN_BLK)
            f_in[n] = source
            b_slot[n] = slot
            prev = jnp.int32(NONE)
            for o in range(EXT):
                hit = slot == o
                prev = jnp.where(hit, f_last[o], prev)
                f_last[o] = jnp.where(hit, n, f_last[o])
            f_prev[n] = prev
            prev = jnp.int32(NONE)
            for o in range(IN_BLK):
                hit = start == o
                prev = jnp.where(hit, b_last[o], prev)
                b_last[o] = jnp.where(hit, n, b_last[o])
            b_prev[n] = prev
        return tuple(f_last + b_last)

    get_rules.wait()
    get_counts.wait()
    ends = lax.fori_loop(0, OFFS, chain, (jnp.int32(NONE),) * (EXT + IN_BLK))
    for o in range(EXT + IN_BLK):
        lasts[o] = ends[o]

    z_pass(False).wait_recv()
    z_pass(True).wait_recv()
    unpack(1)
    for dx, dy in plane:
        send(xy_copy(1, dx, dy))

    def arrive(off, other):
        if other:
            c_copy(off).wait_recv()
        else:
            for dy in range(NY):
                if off or dy:
                    xy_copy(0, (NX - off) % NX, dy).wait_recv()
                    xy_copy(1, (NX - off) % NX, dy).wait_recv()
            send(c_copy(off))

    own_low, own_high = pl.ds(BND, BND), pl.ds(OUT_BLK, BND)
    top, bottom = pl.ds(BND + OUT_BLK, BND), pl.ds(0, BND)
    for t in range(OFFS):
        if t == OFFS // 2 - 1:
            get_cot.wait()
            send(remote(cot.at[own_low], cot.at[top], h_sem, 0, down))
        if t == OFFS // 2:
            send(remote(cot.at[own_high], cot.at[bottom], h_sem, 1, up))
        arrive(order[t // 2], t % 2 == 1)
        picked = [xp[f_in[t * SLOTS + j]] for j in range(SLOTS)]
        products = dot(jnp.concatenate(picked, axis=0), wf[t], NN)
        for j in range(SLOTS):
            n = t * SLOTS + j
            sums[n, :, 0:co] = products[j * br : (j + 1) * br] + sums[f_prev[n]][:, 0:co]

    def rim_copy(i, upward):
        src, dst = (i + OUT_BLK, i) if upward else (i, i + OUT_BLK)
        index = 2 + OUT_BLK * int(upward) + i
        return remote(hs.at[src], hr.at[dst], h_sem, index, up if upward else down)

    for i in range(OUT_BLK):
        for upward in (False, True):
            o = i + OUT_BLK * int(upward)
            hs[o] = sums[lasts[o]].astype(BF16)
            send(rim_copy(i, upward))
    remote(cot.at[own_low], cot.at[top], h_sem, 0, down).wait_recv()
    remote(cot.at[own_high], cot.at[bottom], h_sem, 1, up).wait_recv()
    for i in range(OUT_BLK):
        for upward in (False, True):
            rim_copy(i, upward).wait_recv()
            o = i + (0 if upward else OUT_BLK)
            pre = sums[lasts[o]] + hr[o].astype(F32)
            sigma = 0.5 + 0.5 * jnp.tanh(0.5 * pre)
            if BND <= o < BND + OUT_BLK:
                act_ref[0, (o - BND) * br : (o - BND + 1) * br, :] = (pre * sigma).astype(BF16)
            upstream = cot[o].astype(F32)
            gext[o] = (upstream * sigma * (1.0 + pre * (1.0 - sigma))).astype(BF16)
    put(act_ref, act_hbm, 5)

    def term(off, other):
        t = 2 * order.index(off) + int(other)
        lhs = [xt[f_in[t * SLOTS + j]] for j in range(SLOTS)]
        rhs = [gext[b_slot[t * SLOTS + j]] for j in range(SLOTS)]
        return dot(jnp.concatenate(lhs, axis=1), jnp.concatenate(rhs, axis=0), NN)

    def to_sibling(off):
        sb_send[off] = term(off, True)
        send(remote(sb_send.at[off], sb_recv.at[off], rc_sem, off, sib))

    def part_copy(dx, dy):
        src = xs.at[dx, pl.ds((NY - dy) % NY * part, part)]
        return remote(src, xr.at[dx * NY + dy], rx_sem, dx * NY + dy, at_xy(dx, dy))

    sequence = (2, 1, 3, 0)
    to_sibling(sequence[0])
    for i, off in enumerate(sequence):
        own[...] = term(off, False)
        if i + 1 < NX:
            to_sibling(sequence[i + 1])
        remote(sb_send.at[off], sb_recv.at[off], rc_sem, off, sib).wait_recv()
        own[...] += sb_recv[off]
        xs[off] = own[...].astype(BF16)
        for dy in sorted(range(NY), key=lambda d: -min(d, NY - d)):
            if off or dy:
                send(part_copy(off, dy))

    def back(t):
        picked = [gext[b_slot[t * SLOTS + j]] for j in range(SLOTS)]
        products = dot(jnp.concatenate(picked, axis=0), wf[t], NT)
        for j in range(SLOTS):
            n = t * SLOTS + j
            sums[n, :, 0:ci] = products[j * br : (j + 1) * br] + sums[b_prev[n]][:, 0:ci]

    for t in range(OFFS // 2):
        back(t)

    total = own[0:part, :]
    for dx, dy in plane:
        part_copy(dx, dy).wait_recv()
    for dx, dy in plane:
        total = total + xr[dx * NY + dy].astype(F32)
    for p in range(NZ // 2):
        a, b = total[8 * p : 8 * p + 8, 0:128], total[8 * p : 8 * p + 8, 128:256]
        zs[2 * p] = jnp.where(low, a, pltpu.roll(b, 4, 0))
        zs[2 * p + 1] = jnp.where(low, pltpu.roll(a, 4, 0), b)

    def out_copy(d):
        if d < 2 * REACH:
            tile = d if d < REACH else d + 2 * REACH
        else:
            tile = REACH - 1 + NZ - d
        return remote(zs.at[tile], zr.at[d], rz_sem, d, at_z(d))

    far_first = sorted(range(1, NZ), key=lambda d: -min(d, NZ - d))
    for d in far_first:
        send(out_copy(d))

    for t in range(OFFS // 2, OFFS):
        back(t)
    for i in range(IN_BLK):
        ready = sums[lasts[EXT + i]][:, 0:ci].astype(BF16)
        gf_ref[0, i * br : (i + 1) * br, :] = dot(ready, perm_t, NN).astype(BF16)
    put(gf_ref, gf_hbm, 6)
    for wait in pending:
        wait()
    pending.clear()

    for d in range(1, NZ):
        out_copy(d).wait_recv()

    total = zs[0]
    for d in range(1, NZ):
        total = total + zr[d]
    total = total * grad_scale
    gw_ref[:, 0:128] = total[0:4]
    gw_ref[:, 128:256] = total[4:8]

    put(gw_ref, gw_hbm, 7)
    for wait in pending:
        wait()


def hand_over(act, gf, gw, act_out, gf_out, gw_out, act_here, gf_here, gw_here, sems):
    arrays = ((act, act_here, act_out), (gf, gf_here, gf_out), (gw, gw_here, gw_out))
    into = [pltpu.make_async_copy(a, here, sems.at[0, i]) for i, (a, here, _) in enumerate(arrays)]
    out = [pltpu.make_async_copy(here, b, sems.at[1, i]) for i, (_, here, b) in enumerate(arrays)]
    for copy in into:
        copy.start()
    for first, then in zip(into, out):
        first.wait()
        then.start()
    for copy in out:
        copy.wait()


def local(features, weight, rulebook, rule_counts, cotangent):
    ci, co = features.shape[2], weight.shape[1]
    br = features.shape[1] // IN_BLK
    hbm = pl.BlockSpec(memory_space=pl.ANY)
    rules = jnp.transpose(rulebook, (0, 2, 1, 3))
    dma = pltpu.SemaphoreType.DMA
    V = pltpu.VMEM
    results = pl.pallas_call(
        kernel,
        out_shape=(
            jax.ShapeDtypeStruct(cotangent.shape, BF16),
            jax.ShapeDtypeStruct(features.shape, BF16),
            jax.ShapeDtypeStruct(weight.shape, F32),
        ),
        in_specs=[hbm] * 5,
        out_specs=(hbm, hbm, hbm),
        scratch_shapes=[
            V(features.shape, BF16),
            V(weight.shape, BF16),
            pltpu.SMEM(rules.shape, jnp.int32),
            pltpu.SMEM(rule_counts.shape, jnp.int32),
            V((IN_BLK, br, ci), BF16),
            V((IN_BLK, ci, br), BF16),
            V((EXT, br, co), BF16),
            V((NZ, 8, 128), F32),
            V((4 * NZ, co), F32),
            V((OFFS, ci, co), BF16),
            V((NONE + 1, br, max(ci, co)), F32),
            V((EXT, br, co), BF16),
            V((EXT, br, co), BF16),
            V((EXT + 1, br, co), BF16),
            V(cotangent.shape, BF16),
            V(features.shape, BF16),
            V(weight.shape, F32),
            V((NX, ci, co), F32),
            V((NX, ci, co), F32),
            V((ci, co), F32),
            V((NX, ci, co), BF16),
            V((NX * NY, 4 * NZ, co), BF16),
            V((NZ, 8, 128), F32),
            V((NZ, 8, 128), F32),
            pltpu.SMEM((NONE,), jnp.int32),
            pltpu.SMEM((NONE,), jnp.int32),
            pltpu.SMEM((NONE,), jnp.int32),
            pltpu.SMEM((NONE,), jnp.int32),
            pltpu.SMEM((EXT + IN_BLK,), jnp.int32),
            dma((8,)),
            dma((2, NZ + 2)),
            dma((2, 2 * NX * NY)),
            dma((2, NX)),
            dma((2, 2 + 2 * OUT_BLK)),
            dma((2, NX)),
            dma((2, NX * NY)),
            dma((2, NZ)),
        ],
        compiler_params=pltpu.CompilerParams(
            collective_id=0, has_side_effects=True, vmem_limit_bytes=60 * 1024 * 1024
        ),
    )(features, weight, rules, rule_counts, cotangent.reshape(1, OUT_BLK, br, co))
    return pl.pallas_call(
        hand_over,
        out_shape=tuple(jax.ShapeDtypeStruct(r.shape, r.dtype) for r in results),
        in_specs=[hbm] * 3,
        out_specs=(hbm,) * 3,
        scratch_shapes=[V(r.shape, r.dtype) for r in results] + [dma((2, 3))],
        compiler_params=pltpu.CompilerParams(vmem_limit_bytes=60 * 1024 * 1024),
    )(*results)


def solution(mesh):
    in_specs = (
        P("dp", "space", None),
        P(("dp", "space"), None),
        P("dp", "space", None, None),
        P("dp", "space"),
        P("dp", "space", None),
    )
    out_specs = (P("dp", "space", None), P("dp", "space", None), P(("dp", "space"), None))
    return jax.shard_map(local, mesh=mesh, in_specs=in_specs, out_specs=out_specs, check_vma=False)
```
